512 devices in a mesh: row: 32 (over z_hi, x, core), col: 16 (over z_lo, y).
Axes of the slice: x: 4, y: 8, z: 8 (z_hi: 4, z_lo: 2; z = z_hi * 2 + z_lo), core: 2. Of those that a mesh axis runs over, the one named last changes fastest.
Arguments:
- iterate: bfloat16 [4096, 10240], P('row', 'col'), may hold values from -3.6 to 3.6, as said below
Outputs:
- next_iterate: bfloat16 [4096, 10240], P('row', 'col')
The draws below stay inside these ranges and needn't reach their ends.
Inputs may be any that keep to these rules, and one draw needn't show every extreme that they name: The largest eigenvalue of iterate times its transpose, divided by 10240, is at most about 1.
All inputs are finite; a program needn't handle non-finite values.
Results may differ from the reference program's by a relative error of at most 0.022.
Values may be sent and summed in bfloat16 or wider, within the bound.
No kernel may reach another device: no remote copies, remote signals or barrier semaphores. Data moves between devices by JAX's collectives and lax.ppermute only.
A program may use at most 64 MiB of HBM per device.

```python
import jax
import jax.numpy as jnp
from jax import lax

M = 4096
N = 10240
N_COL = 16


def draw_iterate(key, part):
    key = jax.random.fold_in(key, 11)
    first = jax.random.fold_in(key, 0)
    values = 0.6 * jnp.clip(jax.random.normal(first, (M, N), jnp.float32), -6.0, 6.0)
    return jnp.clip(values, -3.6, 3.6).astype(jnp.bfloat16)


def setup_inputs(seed: int = 0) -> dict:
    key_list = jax.random.split(jax.random.key(seed), 2)
    return {
        "iterate": draw_iterate(jax.random.fold_in(key_list[1], 71), 0),
    }


coef_a = 3.4445
coef_b = -4.7750
coef_c = 2.0315


def reference(iterate):
    blocks = iterate.reshape(M, N_COL, N // N_COL).transpose(1, 0, 2)

    def add_block(total, block):
        part = jnp.dot(block, block.T, preferred_element_type=jnp.float32)
        part = lax.optimization_barrier(part.astype(jnp.bfloat16)).astype(jnp.float32)
        return total + part, None

    total, unused = lax.scan(add_block, jnp.zeros((M, M), jnp.float32), blocks)
    gram = (total / N).astype(jnp.bfloat16)
    image_one = jnp.dot(gram, iterate, preferred_element_type=jnp.float32).astype(jnp.bfloat16)
    image_two = jnp.dot(gram, image_one, preferred_element_type=jnp.float32)
    result = coef_a * iterate.astype(jnp.float32) + coef_b * image_one.astype(jnp.float32) + coef_c * image_two
    return result.astype(jnp.bfloat16)
```

```python
import jax
import jax.numpy as jnp
from jax import lax
from jax.sharding import Mesh, PartitionSpec as P

N = 10240

coef_a = 3.4445
coef_b = -4.775
coef_c = 2.0315

swap = [(0, 1), (1, 0)]


def row_product(left, right):
    return lax.dot_general(
        left, right, (((1,), (1,)), ((), ())), preferred_element_type=jnp.float32
    )


def product(left, right):
    return jnp.dot(left, right, preferred_element_type=jnp.float32)


def both_cores(panel):
    return jnp.concatenate([panel, lax.ppermute(panel, "core", swap)], axis=0)


def sum_pieces(pieces, axes, count):
    rows, columns = pieces.shape
    got = lax.all_to_all(pieces.astype(jnp.bfloat16), axes, 0, 0, tiled=True)
    return jnp.sum(got.reshape(count, rows // count, columns).astype(jnp.float32), axis=0)


def gather(piece, axes, count):
    rows, columns = piece.shape
    copies = jnp.broadcast_to(piece[None], (count, rows, columns))
    return lax.all_to_all(copies.reshape(count * rows, columns), axes, 0, 0, tiled=True)


def on_device(iterate):
    rows_x = lax.all_gather(iterate, "x", axis=0, tiled=True)
    panel = both_cores(lax.all_gather(iterate, "zh", axis=0, tiled=True))
    partial_value = row_product(rows_x, panel)
    total = sum_pieces(partial_value, ("zl", "y"), 16)
    gram = gather((total / N).astype(jnp.bfloat16), ("zl", "y"), 16)
    image_one = sum_pieces(product(gram, panel), "x", 4).astype(jnp.bfloat16)
    panel_one = both_cores(lax.all_gather(image_one, "zh", axis=0, tiled=True))
    image_two = sum_pieces(product(gram, panel_one), "x", 4)
    result = (
        coef_a * iterate.astype(jnp.float32)
        + coef_b * image_one.astype(jnp.float32)
        + coef_c * image_two
    )
    return result.astype(jnp.bfloat16)


def solution(mesh):
    fine = Mesh(mesh.devices.reshape(4, 4, 2, 2, 8), ("zh", "x", "core", "zl", "y"))
    placed = P(("zh", "x", "core"), ("zl", "y"))
    return jax.shard_map(
        on_device, mesh=fine, in_specs=(placed,), out_specs=placed, check_vma=False
    )
```

```python
import jax
import jax.numpy as jnp
from jax import lax
from jax.sharding import Mesh, PartitionSpec as P

N = 10240

coef_a = 3.4445
coef_b = -4.775
coef_c = 2.0315

swap = [(0, 1), (1, 0)]


def row_product(left, right):
    return lax.dot_general(
        left, right, (((1,), (1,)), ((), ())), preferred_element_type=jnp.float32
    )


def product(left, right):
    return jnp.dot(left, right, preferred_element_type=jnp.float32)


def both_cores(panel):
    return jnp.concatenate([panel, lax.ppermute(panel, "core", swap)], axis=0)


def sum_pieces(pieces, axes, count):
    rows, columns = pieces.shape
    got = lax.all_to_all(pieces.astype(jnp.bfloat16), axes, 0, 0, tiled=True)
    return jnp.sum(got.reshape(count, rows // count, columns).astype(jnp.float32), axis=0)


def gather(piece, axes, count):
    rows, columns = piece.shape
    copies = jnp.broadcast_to(piece[None], (count, rows, columns))
    return lax.all_to_all(copies.reshape(count * rows, columns), axes, 0, 0, tiled=True)


def on_device(iterate):
    rows_x = gather(iterate, "x", 4)
    panel = lax.all_gather(iterate, "zh", axis=0, tiled=True)
    rows_x, panel = lax.optimization_barrier((rows_x, panel))
    panel = both_cores(panel)
    partial_value = row_product(rows_x, panel)
    total = sum_pieces(sum_pieces(partial_value, ("zl", "yl"), 4), "yh", 4)
    gram = gather(gather((total / N).astype(jnp.bfloat16), "yh", 4), ("zl", "yl"), 4)
    image_one = sum_pieces(product(gram, panel), "x", 4).astype(jnp.bfloat16)
    panel_one = both_cores(lax.all_gather(image_one, "zh", axis=0, tiled=True))
    image_two = sum_pieces(product(gram, panel_one), "x", 4)
    result = (
        coef_a * iterate.astype(jnp.float32)
        + coef_b * image_one.astype(jnp.float32)
        + coef_c * image_two
    )
    return result.astype(jnp.bfloat16)


def solution(mesh):
    fine = Mesh(mesh.devices.reshape(4, 4, 2, 2, 4, 2), ("zh", "x", "core", "zl", "yh", "yl"))
    placed = P(("zh", "x", "core"), ("zl", "yh", "yl"))
    return jax.shard_map(
        on_device, mesh=fine, in_specs=(placed,), out_specs=placed, check_vma=False
    )
```

```python
import jax
import jax.numpy as jnp
from jax import lax
from jax.sharding import Mesh, PartitionSpec as P

N = 10240

coef_a = 3.4445
coef_b = -4.775
coef_c = 2.0315

swap = [(0, 1), (1, 0)]


def row_product(left, right):
    return lax.dot_general(
        left, right, (((1,), (1,)), ((), ())), preferred_element_type=jnp.float32
    )


def product(left, right):
    return jnp.dot(left, right, preferred_element_type=jnp.float32)


def other_core(panel):
    return lax.ppermute(panel, "core", swap)


def sum_pieces(pieces, axes, count):
    rows, columns = pieces.shape
    got = lax.all_to_all(pieces.astype(jnp.bfloat16), axes, 0, 0, tiled=True)
    return jnp.sum(got.reshape(count, rows // count, columns).astype(jnp.float32), axis=0)


def gather(piece, axes, count):
    rows, columns = piece.shape
    copies = jnp.broadcast_to(piece[None], (count, rows, columns))
    return lax.all_to_all(copies.reshape(count * rows, columns), axes, 0, 0, tiled=True)


def on_device(iterate):
    rows_x = gather(iterate, "x", 4)
    own = lax.all_gather(iterate, "zh", axis=0, tiled=True)
    rows_x, own = lax.optimization_barrier((rows_x, own))
    other = other_core(own)
    partial_value = jnp.concatenate([row_product(rows_x, own), row_product(rows_x, other)], axis=1)
    total = sum_pieces(sum_pieces(partial_value, ("zl", "yl"), 4), "yh", 4)
    gram = gather(gather((total / N).astype(jnp.bfloat16), "yh", 4), ("zl", "yl"), 4)
    image_one = sum_pieces(
        product(gram, jnp.concatenate([own, other], axis=0)), "x", 4
    ).astype(jnp.bfloat16)
    own_one = lax.all_gather(image_one, "zh", axis=0, tiled=True)
    other_one = other_core(own_one)
    image_two = sum_pieces(
        product(gram[:, :512], own_one) + product(gram[:, 512:], other_one), "x", 4
    )
    result = (
        coef_a * iterate.astype(jnp.float32)
        + coef_b * image_one.astype(jnp.float32)
        + coef_c * image_two
    )
    return result.astype(jnp.bfloat16)


def solution(mesh):
    fine = Mesh(mesh.devices.reshape(4, 4, 2, 2, 4, 2), ("zh", "x", "core", "zl", "yh", "yl"))
    placed = P(("zh", "x", "core"), ("zl", "yh", "yl"))
    return jax.shard_map(
        on_device, mesh=fine, in_specs=(placed,), out_specs=placed, check_vma=False
    )
```

```python
import jax
import jax.numpy as jnp
from jax import lax
from jax.sharding import Mesh, PartitionSpec as P

N = 10240

coef_a = 3.4445
coef_b = -4.775
coef_c = 2.0315

swap = [(0, 1), (1, 0)]


def row_product(left, right):
    return lax.dot_general(
        left, right, (((1,), (1,)), ((), ())), preferred_element_type=jnp.float32
    )


def product(left, right):
    return jnp.dot(left, right, preferred_element_type=jnp.float32)


def other_core(panel):
    return lax.ppermute(panel, "core", swap)


def sum_pieces(pieces, axes, count):
    rows, columns = pieces.shape
    got = lax.all_to_all(pieces.astype(jnp.bfloat16), axes, 0, 0, tiled=True)
    return jnp.sum(got.reshape(count, rows // count, columns).astype(jnp.float32), axis=0)


def gather(piece, axes, count):
    rows, columns = piece.shape
    copies = jnp.broadcast_to(piece[None], (count, rows, columns))
    return lax.all_to_all(copies.reshape(count * rows, columns), axes, 0, 0, tiled=True)


def on_device(iterate):
    rows_x = lax.all_gather(iterate, "x", axis=0, tiled=True)
    own = gather(iterate, "zh", 4)
    rows_x, own = lax.optimization_barrier((rows_x, own))
    other = other_core(own)
    partial_value = jnp.concatenate([row_product(rows_x, own), row_product(rows_x, other)], axis=1)
    total = sum_pieces(sum_pieces(partial_value, ("zl", "yl"), 4), "yh", 4)
    gram = gather(gather((total / N).astype(jnp.bfloat16), "yh", 4), ("zl", "yl"), 4)
    image_one = sum_pieces(
        product(gram, jnp.concatenate([own, other], axis=0)), "x", 4
    ).astype(jnp.bfloat16)
    own_one = lax.all_gather(image_one, "zh", axis=0, tiled=True)
    other_one = other_core(own_one)
    image_two = sum_pieces(
        product(gram[:, :512], own_one) + product(gram[:, 512:], other_one), "x", 4
    )
    result = (
        coef_a * iterate.astype(jnp.float32)
        + coef_b * image_one.astype(jnp.float32)
        + coef_c * image_two
    )
    return result.astype(jnp.bfloat16)


def solution(mesh):
    fine = Mesh(mesh.devices.reshape(4, 4, 2, 2, 4, 2), ("zh", "x", "core", "zl", "yh", "yl"))
    placed = P(("zh", "x", "core"), ("zl", "yh", "yl"))
    return jax.shard_map(
        on_device, mesh=fine, in_specs=(placed,), out_specs=placed, check_vma=False
    )
```

```python
import jax
import jax.numpy as jnp
from jax import lax
from jax.sharding import Mesh, PartitionSpec as P

N = 10240

coef_a = 3.4445
coef_b = -4.775
coef_c = 2.0315

swap = [(0, 1), (1, 0)]


def row_product(left, right):
    return lax.dot_general(
        left, right, (((1,), (1,)), ((), ())), preferred_element_type=jnp.float32
    )


def product(left, right):
    return jnp.dot(left, right, preferred_element_type=jnp.float32)


def other_core(panel):
    return lax.ppermute(panel, "core", swap)


def sum_pieces(pieces, axes, count):
    rows, columns = pieces.shape
    got = lax.all_to_all(pieces.astype(jnp.bfloat16), axes, 0, 0, tiled=True)
    got = got.reshape(count, rows // count, columns)
    total = got[0].astype(jnp.float32)
    for i in range(1, count):
        total = total + got[i].astype(jnp.float32)
    return total


def gather(piece, axes, count):
    rows, columns = piece.shape
    copies = jnp.broadcast_to(piece[None], (count, rows, columns))
    return lax.all_to_all(copies.reshape(count * rows, columns), axes, 0, 0, tiled=True)


def on_device(iterate):
    rows_x = lax.all_gather(iterate, "x", axis=0, tiled=True)
    own = gather(iterate, "zh", 4)
    rows_x, own = lax.optimization_barrier((rows_x, own))
    other = other_core(own)
    partial_value = jnp.concatenate([row_product(rows_x, own), row_product(rows_x, other)], axis=1)
    total = sum_pieces(sum_pieces(partial_value, ("zl", "yl"), 4), "yh", 4)
    gram = gather(gather((total / N).astype(jnp.bfloat16), "yh", 4), ("zl", "yl"), 4)
    image_one = sum_pieces(
        product(gram, jnp.concatenate([own, other], axis=0)), "x", 4
    ).astype(jnp.bfloat16)
    own_one = lax.all_gather(image_one, "zh", axis=0, tiled=True)
    other_one = other_core(own_one)
    image_two = sum_pieces(
        product(gram[:, :512], own_one) + product(gram[:, 512:], other_one), "x", 4
    )
    result = (
        coef_a * iterate.astype(jnp.float32)
        + coef_b * image_one.astype(jnp.float32)
        + coef_c * image_two
    )
    return result.astype(jnp.bfloat16)


def solution(mesh):
    fine = Mesh(mesh.devices.reshape(4, 4, 2, 2, 4, 2), ("zh", "x", "core", "zl", "yh", "yl"))
    placed = P(("zh", "x", "core"), ("zl", "yh", "yl"))
    return jax.shard_map(
        on_device, mesh=fine, in_specs=(placed,), out_specs=placed, check_vma=False
    )
```
